32 devices in a mesh: group: 2 (over x), expert: 16 (over z, y, core).
Axes of the slice: x: 2, y: 2, z: 4, core: 2. Of those that a mesh axis runs over, the one named last changes fastest.
Arguments:
- q_latent: bfloat16 [2048, 16384], P(('group', 'expert')), parts along dimension 0
- q_rope: bfloat16 [2048, 4096], P(('group', 'expert')), parts along dimension 0, may hold values from -4 to 4
- latents: bfloat16 [2048, 256], P(('group', 'expert')), parts along dimension 0
- k_rope: bfloat16 [2048, 64], P(('group', 'expert')), parts along dimension 0, may hold values from -6 to 6
- moe_tokens: bfloat16 [512, 3584], P(('group', 'expert')), parts along dimension 0, may hold values from -6 to 6
- routes: int32 [512, 8], P(('group', 'expert')), parts along dimension 0, may hold values from 0 to 15, all different within a row; in each aligned block of 16 rows (0 to 15, 16 to 31, ...) at most 10 rows name the same one
- route_weights: float32 [512, 8], P(('group', 'expert')), parts along dimension 0, may hold values from 0.2 to 1
- w_gate: bfloat16 [16, 3584, 1024], P('expert'), may hold values from -0.09375 to 0.09375
- w_up: bfloat16 [16, 3584, 1024], P('expert'), may hold values from -0.09375 to 0.09375
- w_down: bfloat16 [16, 1024, 3584], P('expert'), may hold values from -0.1875 to 0.1875
Outputs:
- attention_out: bfloat16 [2048, 16384], P(('group', 'expert')), parts along dimension 0
- moe_out: bfloat16 [512, 3584], P(('group', 'expert')), parts along dimension 0
The draws below stay inside these ranges and needn't reach their ends.
There are 2 independent parts, one for each index of `group`. The reference program is written for one: setup_inputs(seed, part) draws one part's arguments, and reference() takes and returns one part's arrays. A program takes and returns all parts, laid end to end along the dimension named above; an argument that names none is the same for every part. Nothing has to cross between parts.
Inputs may be any that keep to these rules, and one draw needn't show every extreme that they name: `routes`: each row names 8 different experts; in each aligned block of 16 rows (the rows of one device) no expert is named by more than 10 rows, a bound that some block reaches.
All inputs are finite; a program needn't handle non-finite values.
Results may differ from the reference program's by a relative error of at most 0.0058.
Values may be sent and summed in bfloat16 or wider, within the bound.
A program may use at most 128 MiB of HBM per device.

```python
import math
import jax
import jax.numpy as jnp
import numpy as np
from jax import lax

D = 3584
HEADS = 64
LATENT = 256
ROPE_DIM = 64
FFN = 1024
TOP = 8
EXPERTS = 16
B_DEV = 16
SPLIT = 1
F_DEV = 1024
CAP = 10
SEQ = 1024
TOKENS_B = 256
N_EXPERT = 16


def shared_latents(key):
    return jax.random.normal(key, (SEQ, LATENT), jnp.float32)


def draw_latents(key, part):
    base_rows = shared_latents(key)
    return base_rows.astype(jnp.bfloat16)


def draw_q_latent(key, part):
    key = jax.random.fold_in(key, 7)
    queries = 0.6 * jax.random.normal(key, (SEQ, HEADS, LATENT), jnp.float32)
    return queries.reshape(SEQ, HEADS * LATENT).astype(jnp.bfloat16)


def block_scale(stream_key, shape, shards, least, high):
    loudness = 1.0
    for axis_at, parts in shards:
        draws = jax.random.uniform(jax.random.fold_in(jax.random.fold_in(stream_key, 6), axis_at), (parts,), jnp.float32, least / len(shards), high / len(shards))
        loudness = loudness * jnp.repeat(jnp.exp(draws), shape[axis_at] // parts).reshape((-1,) + (1,) * (len(shape) - 1 - axis_at))
    return loudness


def assign_block(own_key, own, number, rows, amount, top, limit, lean):
    sequence = jax.random.permutation(own_key, amount)
    crowded, common = portions_of(amount, rows * top, limit, lean, True), portions_of(amount, rows * top, limit, lean, False)
    places = jnp.arange(amount)

    def named(tallies, rotation):
        used = int((tallies > 0).sum())
        fixed = max(1, used // 4)
        passed = fixed + (places - fixed + rotation * (used - fixed)) % max(1, amount - fixed)
        return jnp.zeros((amount,), jnp.int32).at[sequence[jnp.where(places < fixed, places, passed)]].set(jnp.asarray(tallies, jnp.int32))

    tallies = jnp.where(number % 4 == 0, named(crowded, number // 4), named(common, number - number // 4 - 1))
    mixed = jax.random.permutation(jax.random.fold_in(own, 3), amount)
    donor, taker = mixed[0:amount // 2 * 2:2], mixed[1:amount // 2 * 2:2]
    room = jnp.minimum(tallies[donor] - 1, limit - tallies[taker]) // 2
    room = jnp.where((donor == sequence[0]) | (taker == sequence[0]) | (tallies[taker] == 0), 0, jnp.maximum(room, 0))
    passed = jax.random.randint(jax.random.fold_in(own, 4), (amount // 2,), 0, 1 << 20) % (room + 1)
    tallies = tallies.at[donor].add(-passed).at[taker].add(passed)
    members = jnp.searchsorted(jnp.cumsum(tallies), jnp.arange(rows * top), side="right").astype(jnp.int32)
    table = members.reshape(top, rows).T
    table = table[jax.random.permutation(jax.random.fold_in(own, 1), rows)]
    rotation = jax.random.randint(jax.random.fold_in(own, 2), (rows, 1), 0, top)
    return jnp.take_along_axis(table, (jnp.arange(top)[None, :] + rotation) % top, axis=1)


def portions_of(number_of, total, reach, skew, full):
    loads = [(1 << 20) // math.isqrt(standing ** skew) + 1 for standing in range(1, number_of + 1)]
    largest = reach if full else min(reach, max(-(-total // number_of), total * loads[0] // sum(loads)))
    least = 1 if total - largest >= number_of - 1 else 0
    given, rest = [largest] + [least] * (number_of - 1), total - largest - least * (number_of - 1)
    while rest > 0:
        movable = [i for i in range(1, number_of) if given[i] < largest] or [i for i in range(1, number_of) if given[i] < reach]
        whole, budget = sum([loads[i] for i in movable]), rest
        for i in movable:
            more = min(reach - given[i], max(1, budget * loads[i] // whole), rest)
            given[i] = given[i] + more
            rest = rest - more
    return np.array(given)


def gaussian(rng, extent, scale, bound, shards=(), kind=jnp.bfloat16):
    drawn = scale * jax.random.normal(rng, extent, jnp.float32)
    if shards:
        drawn = drawn * block_scale(rng, extent, shards, -0.22, 0.18)
    return jnp.clip(drawn, -bound, bound).astype(kind)


def setup_inputs(seed: int = 0, part: int = 0) -> dict:
    splits = jax.random.split(jax.random.key(seed), 11)
    own_keys = jax.random.split(jax.random.fold_in(splits[10], part), 11)
    q_latent = draw_q_latent(jax.random.fold_in(jax.random.fold_in(splits[10], part), 71), part)
    q_rope = gaussian(own_keys[1], (SEQ, HEADS * ROPE_DIM), 0.6, 4.0, ((0, 16),))
    latents = draw_latents(jax.random.fold_in(jax.random.fold_in(splits[10], part), 71), part)
    k_rope = gaussian(own_keys[3], (SEQ, ROPE_DIM), 1.0, 6.0, ((0, 16),))
    moe_tokens = gaussian(own_keys[4], (TOKENS_B, D), 1.0, 6.0, ((0, 16),))
    routes_keys = jax.random.split(jax.random.fold_in(own_keys[5], 1), TOKENS_B // B_DEV)
    routes_turns = jax.random.permutation(jax.random.fold_in(own_keys[5], 3), TOKENS_B // B_DEV)
    routes = jax.vmap(lambda own, number: assign_block(jax.random.fold_in(own_keys[5], 2), own, number, B_DEV, EXPERTS, TOP, CAP, 2))(routes_keys, routes_turns).reshape((TOKENS_B, TOP))
    route_weights = jnp.clip(0.2 + 0.8 * jax.random.uniform(own_keys[6], (TOKENS_B, TOP), jnp.float32) ** block_scale(own_keys[6], (TOKENS_B, TOP), ((0, 16),), -0.2, 0.2), 0.2, 1.0)
    w_gate = gaussian(splits[7], (N_EXPERT, D, F_DEV), D ** -0.5, 0.09375, ((0, 16),))
    w_up = gaussian(splits[8], (N_EXPERT, D, F_DEV), D ** -0.5, 0.09375, ((0, 16),))
    w_down = gaussian(splits[9], (N_EXPERT, F_DEV, D), FFN ** -0.5, 0.1875, ((0, 16),))
    return dict(q_latent=q_latent, q_rope=q_rope, latents=latents, k_rope=k_rope, moe_tokens=moe_tokens, routes=routes, route_weights=route_weights, w_gate=w_gate, w_up=w_up, w_down=w_down)


SCORE_SCALE = 192.0 ** -0.5
MASKED = -1e30


def head_attention(latents, k_rope, queries):
    lat_query, rope_query = queries
    scores = (jnp.dot(lat_query, latents.T, preferred_element_type=jnp.float32)
              + jnp.dot(rope_query, k_rope.T, preferred_element_type=jnp.float32)) * SCORE_SCALE
    positions = jnp.arange(SEQ, dtype=jnp.int32)
    visible = positions[None, :] <= positions[:, None]
    scores = jnp.where(visible, scores, MASKED)
    row_peak = jnp.max(scores, axis=1, keepdims=True)
    weights_exp = jnp.where(visible, jnp.exp(scores - row_peak), 0.0)
    totals = jnp.sum(weights_exp, axis=1, keepdims=True)
    mixed_out = jnp.dot(weights_exp.astype(jnp.bfloat16), latents, preferred_element_type=jnp.float32)
    return (mixed_out / totals).astype(jnp.bfloat16)


def reference(q_latent, q_rope, latents, k_rope, moe_tokens, routes, route_weights, w_gate, w_up, w_down):
    lat_heads = q_latent.reshape(SEQ, HEADS, LATENT).transpose(1, 0, 2)
    rope_heads = q_rope.reshape(SEQ, HEADS, ROPE_DIM).transpose(1, 0, 2)
    per_head = lax.map(lambda queries: head_attention(latents, k_rope, queries), (lat_heads, rope_heads))
    attention_out = per_head.transpose(1, 0, 2).reshape(SEQ, HEADS * LATENT)

    slot_total = N_EXPERT * CAP
    padded_tokens = jnp.concatenate([moe_tokens, jnp.zeros((1, D), jnp.bfloat16)], axis=0)

    def one_slice(summed, slice_args):
        gate_matrix, up_matrix, down_matrix, slice_id = slice_args
        expert_id = slice_id // SPLIT
        chosen = routes == expert_id
        weight_sum = jnp.sum(jnp.where(chosen, route_weights, 0.0), axis=1)
        is_live = jnp.any(chosen, axis=1)
        row_index = jnp.nonzero(is_live, size=slot_total, fill_value=TOKENS_B)[0].astype(jnp.int32)
        token_rows = padded_tokens[row_index]
        gate_part = jnp.dot(token_rows, gate_matrix, preferred_element_type=jnp.float32)
        up_part = jnp.dot(token_rows, up_matrix, preferred_element_type=jnp.float32)
        hidden_rows = (jax.nn.silu(gate_part) * up_part).astype(jnp.bfloat16)
        part_rows = jnp.dot(hidden_rows, down_matrix, preferred_element_type=jnp.float32).astype(jnp.bfloat16)
        padded_weights = jnp.concatenate([weight_sum, jnp.zeros((1,), weight_sum.dtype)], axis=0)[row_index]
        summed = summed.at[row_index].add(padded_weights[:, None] * part_rows.astype(summed.dtype), mode="drop")
        return summed, 0

    start_sum = jnp.zeros((TOKENS_B, D), jnp.float32)
    slice_ids = jnp.arange(N_EXPERT, dtype=jnp.int32)
    summed, unused = lax.scan(one_slice, start_sum, (w_gate, w_up, w_down, slice_ids))
    moe_out = summed.astype(jnp.bfloat16)
    return attention_out, moe_out
```

```python
import functools

import jax
import jax.numpy as jnp
from jax import lax
from jax.experimental import pallas as pl
from jax.experimental.pallas import tpu as pltpu
from jax.sharding import PartitionSpec as P

LATENT = 256
ROPE_DIM = 64
EXPERTS = 16
LANES = 128

EXP_SCALE = 192.0 ** (-0.5) * 1.4426950408889634
MASKED = -1e30

SIDES = 2
CORES = 2
KEY_WIDTH = LATENT + LANES
PAIRS = 4
ROW_BLOCK = 256
CHUNKS = (1024, 1024, 1024, 512)
EARLY = 4


class Gather:
    def __init__(self, buffer, height, slot_of, device_of, send, recv):
        self.buffer, self.height, self.slot_of, self.device_of = buffer, height, slot_of, device_of
        self.send, self.recv = send, recv
        self.started = []

    def copy(self, place, target, index):
        slot = self.slot_of(*place)
        block = self.buffer.at[pl.ds(pl.multiple_of(slot * self.height, self.height), self.height)]
        return pltpu.make_async_remote_copy(
            src_ref=block,
            dst_ref=block,
            send_sem=self.send.at[index],
            recv_sem=self.recv.at[slot],
            device_id={"expert": self.device_of(*target)},
            device_id_type=pl.DeviceIdType.MESH,
        )

    def start(self, place, target):
        copy = self.copy(place, target, len(self.started))
        copy.start()
        self.started.append(copy)

    def arrive(self, place, target):
        self.copy(place, target, 0).wait_recv()

    def finish(self):
        for copy in self.started:
            copy.wait_send()


def kernel(
    n,
    split,
    q_lat,
    q_rope,
    latents,
    k_rope,
    tokens,
    routes,
    route_weights,
    w_gate,
    w_up,
    w_down,
    att_out,
    moe_out,
    keys,
    toks,
    part,
    from_core,
    from_side,
    from_line,
    kt_even,
    kt_odd,
    hidden,
    gate,
    up,
    down,
    weight_sem,
    keys_send,
    keys_recv,
    toks_send,
    toks_recv,
    core_send,
    core_recv,
    side_send,
    side_recv,
    line_send,
    line_recv,
):
    count = n // (SIDES * CORES)
    queries = q_lat.shape[0]
    token_count, width = tokens.shape
    f_dev = gate.shape[1]
    all_keys = keys.shape[0]
    all_tokens = toks.shape[0]
    me = lax.axis_index("expert")
    core, side, line = me % CORES, (me // CORES) % SIDES, me // (SIDES * CORES)
    mine = (line, side, core)
    sibling = (line, side, 1 - core)
    across = (line, 1 - side, core)
    if count == 4:
        others = [line + 1 - 2 * (line % 2), (line + 2) % 4, 3 - line]
    else:
        others = [(line + k) % count for k in range(1, count)]

    def device_of(line, side, core):
        return (line * SIDES + side) * CORES + core

    def token_slot(line, side, core):
        return (core * SIDES + side) * count + line

    weight_copies = [
        pltpu.make_async_copy(w_gate.at[0], gate, weight_sem.at[0]),
        pltpu.make_async_copy(w_up.at[0], up, weight_sem.at[1]),
        pltpu.make_async_copy(w_down.at[0], down, weight_sem.at[2]),
    ]
    for copy in weight_copies:
        copy.start()

    barrier = pltpu.get_barrier_semaphore()
    partners = [sibling, across] + [(other, side, core) for other in others]
    for partner in partners:
        pl.semaphore_signal(
            barrier,
            inc=1,
            device_id={"expert": device_of(*partner)},
            device_id_type=pl.DeviceIdType.MESH,
        )

    key_rows = pl.ds(pl.multiple_of(me * queries, queries), queries)
    keys[key_rows, :LATENT] = latents[...]
    keys[key_rows, LATENT:] = jnp.concatenate(
        [k_rope[...], jnp.zeros((queries, LANES - ROPE_DIM), jnp.bfloat16)], axis=1
    )
    my_token_slot = token_slot(*mine)
    token_rows = pl.ds(pl.multiple_of(my_token_slot * token_count, token_count), token_count)
    toks[token_rows, :width] = tokens[...]
    lane = lax.broadcasted_iota(jnp.int32, (token_count, LANES), 1)
    dense = jnp.zeros((token_count, LANES), jnp.float32)
    for k in range(routes.shape[1]):
        dense = dense + jnp.where(routes[:, k : k + 1] == lane, route_weights[:, k : k + 1], 0.0)
    dense_high = dense.astype(jnp.bfloat16)
    dense_low = (dense - dense_high.astype(jnp.float32)).astype(jnp.bfloat16)
    toks[token_rows, width : width + LANES] = dense_high
    toks[token_rows, width + LANES :] = dense_low

    pl.semaphore_wait(barrier, len(partners))

    key_gather = Gather(keys, queries, device_of, device_of, keys_send, keys_recv)
    tok_gather = Gather(toks, token_count, token_slot, device_of, toks_send, toks_recv)
    for gather in (key_gather, tok_gather):
        gather.start(mine, across)
        for other in others:
            gather.start(mine, (other, side, core))
        gather.start(mine, sibling)

    def forward_line(gather, other):
        place = (other, side, core)
        gather.arrive(place, sibling)
        gather.start(place, across)
        gather.start(place, sibling)

    def forward_side(gather, other):
        place = (other, 1 - side, core)
        gather.arrive(place, sibling)
        gather.start(place, sibling)

    def last_arrivals(gather):
        for other in [line] + others:
            for s in range(SIDES):
                gather.arrive((other, s, 1 - core), sibling)

    for other in others:
        forward_line(key_gather, other)
    for other in [line] + others:
        forward_side(key_gather, other)
    last_arrivals(key_gather)

    first = me * queries
    zero_rows = jnp.zeros((ROPE_DIM, ROW_BLOCK), jnp.bfloat16)
    for start in range(0, all_keys, ROW_BLOCK):
        cols = slice(start, start + ROW_BLOCK)
        turned = jnp.transpose(keys[cols, :])
        kt_even[:KEY_WIDTH, cols] = turned
        kt_odd[:LATENT, cols] = turned[:LATENT]
        kt_odd[LATENT : LATENT + ROPE_DIM, cols] = zero_rows
        kt_odd[LATENT + ROPE_DIM : KEY_WIDTH, cols] = turned[LATENT : LATENT + ROPE_DIM]
        row = lax.broadcasted_iota(jnp.int32, (LANES, ROW_BLOCK), 0)
        key = lax.broadcasted_iota(jnp.int32, (LANES, ROW_BLOCK), 1) + start
        mask = jnp.where(key > first + row, MASKED, 0.0).astype(jnp.bfloat16)
        kt_even[KEY_WIDTH:, cols] = mask
        kt_odd[KEY_WIDTH:, cols] = mask

    picks = jnp.where(
        lax.broadcasted_iota(jnp.int32, (queries, LANES), 0)
        == lax.broadcasted_iota(jnp.int32, (queries, LANES), 1),
        1.0,
        0.0,
    ).astype(jnp.bfloat16)

    def attend(step, carry):
        for odd, kt in ((0, kt_even), (1, kt_odd)):
            rows = []
            heads = []
            for p in range(PAIRS):
                pair = step * PAIRS + p
                head = pl.ds(pl.multiple_of((2 * pair + odd) * LATENT, LATENT), LATENT)
                ropes = pl.ds(pl.multiple_of(pair * LANES, LANES), LANES)
                heads.append(head)
                rows.append(jnp.concatenate([q_lat[:, head], q_rope[:, ropes], picks], axis=1))
            scores = jnp.dot(
                jnp.concatenate(rows, axis=0), kt[...], preferred_element_type=jnp.float32
            )
            peak = jnp.max(scores, axis=1, keepdims=True)
            weights = jnp.exp2((scores - peak) * EXP_SCALE)
            totals = jnp.sum(weights, axis=1, keepdims=True)
            mixed = jnp.dot(
                weights.astype(jnp.bfloat16),
                keys[:, :LATENT],
                preferred_element_type=jnp.float32,
            )
            mixed = (mixed / totals).astype(jnp.bfloat16)
            for p in range(PAIRS):
                att_out[:, heads[p]] = mixed[p * queries : (p + 1) * queries]
        return carry

    steps = q_lat.shape[1] // (2 * PAIRS * LATENT)

    def attend_some(low, high):
        lax.fori_loop(low, high, attend, 0)

    early = min(EARLY, steps)
    for at, other in enumerate(others):
        if at < early:
            attend_some(at, at + 1)
        forward_line(tok_gather, other)
    done = min(len(others), early)
    attend_some(done, early)
    for other in [line] + others:
        forward_side(tok_gather, other)
    last_arrivals(tok_gather)
    weight_copies[0].wait()
    weight_copies[1].wait()

    expert = me // split
    blocks = all_tokens // ROW_BLOCK

    def gate_up(at, carry):
        rows = pl.ds(pl.multiple_of((at % blocks) * ROW_BLOCK, ROW_BLOCK), ROW_BLOCK)
        cols = pl.ds(pl.multiple_of((at // blocks) * 256, 256), 256)
        x = toks[rows, :width]
        g = jnp.dot(x, gate[:, cols], preferred_element_type=jnp.float32)
        u = jnp.dot(x, up[:, cols], preferred_element_type=jnp.float32)
        hidden[rows, cols] = (g / (1.0 + jnp.exp(-g)) * u).astype(jnp.bfloat16)
        return carry

    lax.fori_loop(0, blocks * (f_dev // 256), gate_up, 0)
    weight_copies[2].wait()

    half, quarter = all_tokens // 2, all_tokens // 4
    near_half = pl.ds(pl.multiple_of(core * half, half), half)
    far_half = pl.ds(pl.multiple_of((1 - core) * half, half), half)
    near_quarter = pl.ds(pl.multiple_of(core * half + side * quarter, quarter), quarter)
    far_quarter = pl.ds(pl.multiple_of(core * half + (1 - side) * quarter, quarter), quarter)
    spans = []
    at = 0
    for size in CHUNKS:
        spans.append(slice(at, at + size))
        at += size
    started = []

    def remote(src, dst, send, recv, target):
        return pltpu.make_async_remote_copy(
            src_ref=src,
            dst_ref=dst,
            send_sem=send,
            recv_sem=recv,
            device_id={"expert": device_of(*target)},
            device_id_type=pl.DeviceIdType.MESH,
        )

    def core_copy(j):
        return remote(
            part.at[far_half, spans[j]],
            from_core.at[:, spans[j]],
            core_send.at[j],
            core_recv.at[j],
            sibling,
        )

    def side_copy(j):
        return remote(
            part.at[far_quarter, spans[j]],
            from_side.at[:, spans[j]],
            side_send.at[j],
            side_recv.at[j],
            across,
        )

    def line_rows(line):
        slot = token_slot(line, side, core)
        return pl.ds(pl.multiple_of(slot * token_count, token_count), token_count)

    def line_slot(line):
        return pl.ds(pl.multiple_of(line * token_count, token_count), token_count)

    def line_copy(j, k, owner):
        return remote(
            part.at[line_rows(others[k]), spans[j]],
            from_line.at[line_slot(owner), spans[j]],
            line_send.at[j * len(others) + k],
            line_recv.at[j * count + owner],
            (others[k], side, core),
        )

    def begin(copy):
        copy.start()
        started.append(copy)

    def produce(j):
        def one(at, carry):
            rows = pl.ds(pl.multiple_of(at * ROW_BLOCK, ROW_BLOCK), ROW_BLOCK)
            lanes = lax.broadcasted_iota(jnp.int32, (ROW_BLOCK, LANES), 1)
            both = toks[rows, width : width + LANES].astype(jnp.float32) + toks[
                rows, width + LANES :
            ].astype(jnp.float32)
            scale = jnp.sum(jnp.where(lanes == expert, both, 0.0), axis=1, keepdims=True)
            out = jnp.dot(hidden[rows, :], down[:, spans[j]], preferred_element_type=jnp.float32)
            part[rows, spans[j]] = (out * scale).astype(jnp.bfloat16)
            return carry

        lax.fori_loop(0, blocks, one, 0)
        begin(core_copy(j))

    def join_core(j):
        core_copy(j).wait_recv()
        summed = part[near_half, spans[j]].astype(jnp.float32) + from_core[:, spans[j]].astype(
            jnp.float32
        )
        part[near_half, spans[j]] = summed.astype(jnp.bfloat16)
        begin(side_copy(j))

    def join_side(j):
        side_copy(j).wait_recv()
        summed = part[near_quarter, spans[j]].astype(jnp.float32) + from_side[
            :, spans[j]
        ].astype(jnp.float32)
        part[near_quarter, spans[j]] = summed.astype(jnp.bfloat16)
        for k in range(len(others)):
            begin(line_copy(j, k, line))

    def join_line(j):
        summed = part[line_rows(line), spans[j]].astype(jnp.float32)
        for k, other in enumerate(others):
            line_copy(j, k, other).wait_recv()
            summed = summed + from_line[line_slot(other), spans[j]].astype(jnp.float32)
        moe_out[:, spans[j]] = summed.astype(jnp.bfloat16)

    parts = len(spans)
    for j in range(parts):
        produce(j)
        if j:
            join_core(j - 1)
    join_core(parts - 1)
    left = steps - early
    for j in range(parts):
        attend_some(early + left * j // parts, early + left * (j + 1) // parts)
        join_side(j)
    for j in range(parts):
        join_line(j)
    key_gather.finish()
    tok_gather.finish()
    for copy in started:
        copy.wait_send()


def per_device(
    q_latent, q_rope, latents, k_rope, moe_tokens, routes, route_weights, w_gate, w_up, w_down
):
    n = lax.axis_size("expert")
    queries = latents.shape[0]
    token_count, width = moe_tokens.shape
    f_dev = w_gate.shape[2]
    count = n // (SIDES * CORES)
    all_tokens = n * token_count
    vmem = pl.BlockSpec(memory_space=pltpu.VMEM)
    hbm = pl.BlockSpec(memory_space=pl.ANY)
    bf16 = jnp.bfloat16
    parts = len(CHUNKS)
    dma = pltpu.SemaphoreType.DMA
    return pl.pallas_call(
        functools.partial(kernel, n, n // EXPERTS),
        out_shape=(
            jax.ShapeDtypeStruct(q_latent.shape, bf16),
            jax.ShapeDtypeStruct(moe_tokens.shape, bf16),
        ),
        in_specs=[vmem] * 7 + [hbm] * 3,
        out_specs=(vmem, vmem),
        scratch_shapes=[
            pltpu.VMEM((n * queries, KEY_WIDTH), bf16),
            pltpu.VMEM((all_tokens, width + 2 * LANES), bf16),
            pltpu.VMEM((all_tokens, width), bf16),
            pltpu.VMEM((all_tokens // 2, width), bf16),
            pltpu.VMEM((all_tokens // 4, width), bf16),
            pltpu.VMEM((count * token_count, width), bf16),
            pltpu.VMEM((KEY_WIDTH + LANES, n * queries), bf16),
            pltpu.VMEM((KEY_WIDTH + LANES, n * queries), bf16),
            pltpu.VMEM((all_tokens, f_dev), bf16),
            pltpu.VMEM((width, f_dev), bf16),
            pltpu.VMEM((width, f_dev), bf16),
            pltpu.VMEM((f_dev, width), bf16),
            dma((3,)),
            dma((n - 1,)),
            dma((n,)),
            dma((n - 1,)),
            dma((n,)),
            dma((parts,)),
            dma((parts,)),
            dma((parts,)),
            dma((parts,)),
            dma((parts * (count - 1),)),
            dma((parts * count,)),
        ],
        compiler_params=pltpu.CompilerParams(
            collective_id=0, has_side_effects=True, vmem_limit_bytes=60 * 1024 * 1024
        ),
        cost_estimate=pl.CostEstimate(
            flops=2 * 4096 * 1024 * 768, bytes_accessed=30_000_000, transcendentals=4096 * 1024
        ),
    )(q_latent, q_rope, latents, k_rope, moe_tokens, routes, route_weights, w_gate, w_up, w_down)


def solution(mesh):
    rows = P(("group", "expert"), None)
    stacks = P("expert", None, None)
    return jax.shard_map(
        per_device,
        mesh=mesh,
        in_specs=(rows,) * 7 + (stacks,) * 3,
        out_specs=(rows, rows),
        check_vma=False,
    )
```

```python
import functools

import jax
import jax.numpy as jnp
from jax import lax
from jax.experimental import pallas as pl
from jax.experimental.pallas import tpu as pltpu
from jax.sharding import PartitionSpec as P

LATENT = 256
ROPE_DIM = 64
EXPERTS = 16
LANES = 128

EXP_SCALE = 192.0 ** (-0.5) * 1.4426950408889634
MASKED = -1e30

SIDES = 2
CORES = 2
KEY_WIDTH = LATENT + LANES
PAIRS = 4
ROW_BLOCK = 256
CHUNKS = (1024, 1024, 1024, 512)


class Gather:
    def __init__(self, buffer, height, slot_of, device_of, send, recv):
        self.buffer, self.height, self.slot_of, self.device_of = buffer, height, slot_of, device_of
        self.send, self.recv = send, recv
        self.started = []

    def copy(self, place, target, index):
        slot = self.slot_of(*place)
        block = self.buffer.at[pl.ds(pl.multiple_of(slot * self.height, self.height), self.height)]
        return pltpu.make_async_remote_copy(
            src_ref=block,
            dst_ref=block,
            send_sem=self.send.at[index],
            recv_sem=self.recv.at[slot],
            device_id={"expert": self.device_of(*target)},
            device_id_type=pl.DeviceIdType.MESH,
        )

    def start(self, place, target):
        copy = self.copy(place, target, len(self.started))
        copy.start()
        self.started.append(copy)

    def arrive(self, place, target):
        self.copy(place, target, 0).wait_recv()

    def finish(self):
        for copy in self.started:
            copy.wait_send()


def kernel(
    n,
    split,
    q_lat_hbm,
    q_rope_hbm,
    latents,
    k_rope,
    tokens,
    routes,
    route_weights,
    w_gate,
    w_up,
    w_down,
    att_out,
    moe_out,
    keys,
    toks,
    part,
    from_core,
    from_side,
    from_line,
    kt_even,
    kt_odd,
    hidden,
    gate,
    up,
    down,
    q_lat,
    q_rope,
    weight_sem,
    keys_send,
    keys_recv,
    toks_send,
    toks_recv,
    core_send,
    core_recv,
    side_send,
    side_recv,
    line_send,
    line_recv,
):
    count = n // (SIDES * CORES)
    queries = q_lat.shape[0]
    token_count, width = tokens.shape
    f_dev = gate.shape[1]
    all_keys = keys.shape[0]
    all_tokens = toks.shape[0]
    me = lax.axis_index("expert")
    core, side, line = me % CORES, (me // CORES) % SIDES, me // (SIDES * CORES)
    mine = (line, side, core)
    sibling = (line, side, 1 - core)
    across = (line, 1 - side, core)
    if count == 4:
        others = [line + 1 - 2 * (line % 2), (line + 2) % 4, 3 - line]
    else:
        others = [(line + k) % count for k in range(1, count)]

    def device_of(line, side, core):
        return (line * SIDES + side) * CORES + core

    def token_slot(line, side, core):
        return (core * SIDES + side) * count + line

    weight_copies = [
        pltpu.make_async_copy(w_gate.at[0], gate, weight_sem.at[0]),
        pltpu.make_async_copy(w_up.at[0], up, weight_sem.at[1]),
        pltpu.make_async_copy(w_down.at[0], down, weight_sem.at[2]),
    ]
    query_copies = [
        pltpu.make_async_copy(q_lat_hbm, q_lat, weight_sem.at[3]),
        pltpu.make_async_copy(q_rope_hbm, q_rope, weight_sem.at[4]),
    ]
    for copy in weight_copies + query_copies:
        copy.start()

    barrier = pltpu.get_barrier_semaphore()
    partners = [sibling, across] + [(other, side, core) for other in others]
    for partner in partners:
        pl.semaphore_signal(
            barrier,
            inc=1,
            device_id={"expert": device_of(*partner)},
            device_id_type=pl.DeviceIdType.MESH,
        )

    key_rows = pl.ds(pl.multiple_of(me * queries, queries), queries)
    keys[key_rows, :LATENT] = latents[...]
    keys[key_rows, LATENT:] = jnp.concatenate(
        [k_rope[...], jnp.zeros((queries, LANES - ROPE_DIM), jnp.bfloat16)], axis=1
    )
    my_token_slot = token_slot(*mine)
    token_rows = pl.ds(pl.multiple_of(my_token_slot * token_count, token_count), token_count)
    toks[token_rows, :width] = tokens[...]
    lane = lax.broadcasted_iota(jnp.int32, (token_count, LANES), 1)
    dense = jnp.zeros((token_count, LANES), jnp.float32)
    picked = jnp.transpose(routes[...])
    amounts = jnp.transpose(route_weights[...])
    for k in range(picked.shape[1]):
        dense = dense + jnp.where(picked[:, k : k + 1] == lane, amounts[:, k : k + 1], 0.0)
    dense_high = dense.astype(jnp.bfloat16)
    dense_low = (dense - dense_high.astype(jnp.float32)).astype(jnp.bfloat16)
    toks[token_rows, width : width + LANES] = dense_high
    toks[token_rows, width + LANES :] = dense_low

    pl.semaphore_wait(barrier, len(partners))

    key_gather = Gather(keys, queries, device_of, device_of, keys_send, keys_recv)
    tok_gather = Gather(toks, token_count, token_slot, device_of, toks_send, toks_recv)

    def send_own(gather):
        gather.start(mine, across)
        for other in others:
            gather.start(mine, (other, side, core))
        gather.start(mine, sibling)

    def forward_line(gather, other):
        place = (other, side, core)
        gather.arrive(place, sibling)
        gather.start(place, across)
        gather.start(place, sibling)

    def forward_side(gather, other):
        place = (other, 1 - side, core)
        gather.arrive(place, sibling)
        gather.start(place, sibling)

    def last_arrivals(gather):
        for other in [line] + others:
            for s in range(SIDES):
                gather.arrive((other, s, 1 - core), sibling)

    send_own(tok_gather)
    for other in others:
        forward_line(tok_gather, other)
    send_own(key_gather)
    for other in [line] + others:
        forward_side(tok_gather, other)
    last_arrivals(tok_gather)
    weight_copies[0].wait()
    weight_copies[1].wait()

    picks = jnp.where(
        lax.broadcasted_iota(jnp.int32, (queries, LANES), 0)
        == lax.broadcasted_iota(jnp.int32, (queries, LANES), 1),
        1.0,
        0.0,
    ).astype(jnp.bfloat16)

    def attend(step, carry):
        for odd, kt in ((0, kt_even), (1, kt_odd)):
            rows = []
            heads = []
            for p in range(PAIRS):
                pair = step * PAIRS + p
                head = pl.ds(pl.multiple_of((2 * pair + odd) * LATENT, LATENT), LATENT)
                ropes = pl.ds(pl.multiple_of(pair * LANES, LANES), LANES)
                heads.append(head)
                rows.append(jnp.concatenate([q_lat[:, head], q_rope[:, ropes], picks], axis=1))
            scores = jnp.dot(
                jnp.concatenate(rows, axis=0), kt[...], preferred_element_type=jnp.float32
            )
            peak = jnp.max(scores, axis=1, keepdims=True)
            weights = jnp.exp2((scores - peak) * EXP_SCALE)
            totals = jnp.sum(weights, axis=1, keepdims=True)
            mixed = jnp.dot(
                weights.astype(jnp.bfloat16),
                keys[:, :LATENT],
                preferred_element_type=jnp.float32,
            )
            mixed = (mixed / totals).astype(jnp.bfloat16)
            for p in range(PAIRS):
                att_out[:, heads[p]] = mixed[p * queries : (p + 1) * queries]
        return carry

    steps = q_lat.shape[1] // (2 * PAIRS * LATENT)

    def attend_some(low, high):
        lax.fori_loop(low, high, attend, 0)

    expert = me // split
    blocks = all_tokens // ROW_BLOCK

    def gate_up(at, carry):
        rows = pl.ds(pl.multiple_of((at % blocks) * ROW_BLOCK, ROW_BLOCK), ROW_BLOCK)
        cols = pl.ds(pl.multiple_of((at // blocks) * 256, 256), 256)
        x = toks[rows, :width]
        g = jnp.dot(x, gate[:, cols], preferred_element_type=jnp.float32)
        u = jnp.dot(x, up[:, cols], preferred_element_type=jnp.float32)
        hidden[rows, cols] = (g / (1.0 + jnp.exp(-g)) * u).astype(jnp.bfloat16)
        return carry

    tiles = blocks * (f_dev // 256)
    lax.fori_loop(0, tiles // 2, gate_up, 0)
    for other in others:
        forward_line(key_gather, other)
    lax.fori_loop(tiles // 2, tiles, gate_up, 0)
    for other in [line] + others:
        forward_side(key_gather, other)
    weight_copies[2].wait()

    half, quarter = all_tokens // 2, all_tokens // 4
    near_half = pl.ds(pl.multiple_of(core * half, half), half)
    far_half = pl.ds(pl.multiple_of((1 - core) * half, half), half)
    near_quarter = pl.ds(pl.multiple_of(core * half + side * quarter, quarter), quarter)
    far_quarter = pl.ds(pl.multiple_of(core * half + (1 - side) * quarter, quarter), quarter)
    spans = []
    at = 0
    for size in CHUNKS:
        spans.append(slice(at, at + size))
        at += size
    started = []

    def remote(src, dst, send, recv, target):
        return pltpu.make_async_remote_copy(
            src_ref=src,
            dst_ref=dst,
            send_sem=send,
            recv_sem=recv,
            device_id={"expert": device_of(*target)},
            device_id_type=pl.DeviceIdType.MESH,
        )

    def core_copy(j):
        return remote(
            part.at[far_half, spans[j]],
            from_core.at[:, spans[j]],
            core_send.at[j],
            core_recv.at[j],
            sibling,
        )

    def side_copy(j):
        return remote(
            part.at[far_quarter, spans[j]],
            from_side.at[:, spans[j]],
            side_send.at[j],
            side_recv.at[j],
            across,
        )

    def line_rows(line):
        slot = token_slot(line, side, core)
        return pl.ds(pl.multiple_of(slot * token_count, token_count), token_count)

    def line_slot(line):
        return pl.ds(pl.multiple_of(line * token_count, token_count), token_count)

    def line_copy(j, k, owner):
        return remote(
            part.at[line_rows(others[k]), spans[j]],
            from_line.at[line_slot(owner), spans[j]],
            line_send.at[j * len(others) + k],
            line_recv.at[j * count + owner],
            (others[k], side, core),
        )

    def begin(copy):
        copy.start()
        started.append(copy)

    def produce(j):
        def one(at, carry):
            rows = pl.ds(pl.multiple_of(at * ROW_BLOCK, ROW_BLOCK), ROW_BLOCK)
            lanes = lax.broadcasted_iota(jnp.int32, (ROW_BLOCK, LANES), 1)
            both = toks[rows, width : width + LANES].astype(jnp.float32) + toks[
                rows, width + LANES :
            ].astype(jnp.float32)
            scale = jnp.sum(jnp.where(lanes == expert, both, 0.0), axis=1, keepdims=True)
            out = jnp.dot(hidden[rows, :], down[:, spans[j]], preferred_element_type=jnp.float32)
            part[rows, spans[j]] = (out * scale).astype(jnp.bfloat16)
            return carry

        lax.fori_loop(0, blocks, one, 0)
        begin(core_copy(j))

    def join_core(j):
        core_copy(j).wait_recv()
        summed = part[near_half, spans[j]].astype(jnp.float32) + from_core[:, spans[j]].astype(
            jnp.float32
        )
        part[near_half, spans[j]] = summed.astype(jnp.bfloat16)
        begin(side_copy(j))

    def join_side(j):
        side_copy(j).wait_recv()
        summed = part[near_quarter, spans[j]].astype(jnp.float32) + from_side[
            :, spans[j]
        ].astype(jnp.float32)
        part[near_quarter, spans[j]] = summed.astype(jnp.bfloat16)
        for k in range(len(others)):
            begin(line_copy(j, k, line))

    def join_line(j):
        summed = part[line_rows(line), spans[j]].astype(jnp.float32)
        for k, other in enumerate(others):
            line_copy(j, k, other).wait_recv()
            summed = summed + from_line[line_slot(other), spans[j]].astype(jnp.float32)
        moe_out[:, spans[j]] = summed.astype(jnp.bfloat16)

    parts = len(spans)
    for j in range(parts):
        produce(j)
        if j:
            join_core(j - 1)
    join_core(parts - 1)
    last_arrivals(key_gather)
    for copy in query_copies:
        copy.wait()

    first = me * queries
    zero_rows = jnp.zeros((ROPE_DIM, ROW_BLOCK), jnp.bfloat16)
    for start in range(0, all_keys, ROW_BLOCK):
        cols = slice(start, start + ROW_BLOCK)
        turned = jnp.transpose(keys[cols, :])
        kt_even[:KEY_WIDTH, cols] = turned
        kt_odd[:LATENT, cols] = turned[:LATENT]
        kt_odd[LATENT : LATENT + ROPE_DIM, cols] = zero_rows
        kt_odd[LATENT + ROPE_DIM : KEY_WIDTH, cols] = turned[LATENT : LATENT + ROPE_DIM]
        row = lax.broadcasted_iota(jnp.int32, (LANES, ROW_BLOCK), 0)
        key = lax.broadcasted_iota(jnp.int32, (LANES, ROW_BLOCK), 1) + start
        mask = jnp.where(key > first + row, MASKED, 0.0).astype(jnp.bfloat16)
        kt_even[KEY_WIDTH:, cols] = mask
        kt_odd[KEY_WIDTH:, cols] = mask

    for j in range(parts):
        attend_some(steps * j // (parts + 1), steps * (j + 1) // (parts + 1))
        join_side(j)
    attend_some(steps * parts // (parts + 1), steps)
    for j in range(parts):
        join_line(j)
    key_gather.finish()
    tok_gather.finish()
    for copy in started:
        copy.wait_send()


def per_device(
    q_latent, q_rope, latents, k_rope, moe_tokens, routes, route_weights, w_gate, w_up, w_down
):
    n = lax.axis_size("expert")
    queries = latents.shape[0]
    token_count, width = moe_tokens.shape
    f_dev = w_gate.shape[2]
    count = n // (SIDES * CORES)
    all_tokens = n * token_count
    vmem = pl.BlockSpec(memory_space=pltpu.VMEM)
    hbm = pl.BlockSpec(memory_space=pl.ANY)
    bf16 = jnp.bfloat16
    parts = len(CHUNKS)
    dma = pltpu.SemaphoreType.DMA
    return pl.pallas_call(
        functools.partial(kernel, n, n // EXPERTS),
        out_shape=(
            jax.ShapeDtypeStruct(q_latent.shape, bf16),
            jax.ShapeDtypeStruct(moe_tokens.shape, bf16),
        ),
        in_specs=[hbm] * 2 + [vmem] * 5 + [hbm] * 3,
        out_specs=(vmem, vmem),
        scratch_shapes=[
            pltpu.VMEM((n * queries, KEY_WIDTH), bf16),
            pltpu.VMEM((all_tokens, width + 2 * LANES), bf16),
            pltpu.VMEM((all_tokens, width), bf16),
            pltpu.VMEM((all_tokens // 2, width), bf16),
            pltpu.VMEM((all_tokens // 4, width), bf16),
            pltpu.VMEM((count * token_count, width), bf16),
            pltpu.VMEM((KEY_WIDTH + LANES, n * queries), bf16),
            pltpu.VMEM((KEY_WIDTH + LANES, n * queries), bf16),
            pltpu.VMEM((all_tokens, f_dev), bf16),
            pltpu.VMEM((width, f_dev), bf16),
            pltpu.VMEM((width, f_dev), bf16),
            pltpu.VMEM((f_dev, width), bf16),
            pltpu.VMEM(q_latent.shape, bf16),
            pltpu.VMEM((queries, q_latent.shape[1] // LATENT * ROPE_DIM), bf16),
            dma((5,)),
            dma((n - 1,)),
            dma((n,)),
            dma((n - 1,)),
            dma((n,)),
            dma((parts,)),
            dma((parts,)),
            dma((parts,)),
            dma((parts,)),
            dma((parts * (count - 1),)),
            dma((parts * count,)),
        ],
        compiler_params=pltpu.CompilerParams(
            collective_id=0, has_side_effects=True, vmem_limit_bytes=60 * 1024 * 1024
        ),
        cost_estimate=pl.CostEstimate(
            flops=2 * 4096 * 1024 * 768, bytes_accessed=30_000_000, transcendentals=4096 * 1024
        ),
    )(
        q_latent,
        q_rope,
        latents,
        k_rope,
        moe_tokens,
        routes.T,
        route_weights.T,
        w_gate,
        w_up,
        w_down,
    )


def solution(mesh):
    rows = P(("group", "expert"), None)
    stacks = P("expert", None, None)
    return jax.shard_map(
        per_device,
        mesh=mesh,
        in_specs=(rows,) * 7 + (stacks,) * 3,
        out_specs=(rows, rows),
        check_vma=False,
    )
```
